32 devices in a mesh: cells: 8 (over z, y), freq: 4 (over x, core).
Axes of the slice: x: 2, y: 2, z: 4, core: 2. Of those that a mesh axis runs over, the one named last changes fastest.
Arguments:
- adj_source: float32 [4, 2, 32768], P('freq', None, 'cells'), may hold values from -6 to 6
- contrast: float32 [4, 32768], P('freq', 'cells'), may hold values from 0.2 to 0.8
- background: float32 [4, 2, 32768], P('freq', None, 'cells'), may hold values from -6 to 6
- near_blocks: float32 [4, 2, 192, 32768], P('freq', None, None, 'cells'), may hold values from -0.3125 to 0.3125
- near_list: int32 [512, 3], P('cells'), may hold values from 0 to 511, as said below
- proj_basis: float32 [4, 2, 16, 32768], P('freq', None, None, 'cells'), may hold values from -0.5 to 0.5
- expand_basis: float32 [4, 2, 16, 32768], P('freq', None, None, 'cells'), may hold values from -1 to 1
- coupling: float32 [4, 2, 16, 16, 8192], P('freq', None, None, None, 'cells'), may hold values from -0.25 to 0.25
- far_owner: int32 [8192, 1], P('cells'), may hold values from 0 to 7; in each aligned block of 1024 rows (0 to 1023, 1024 to 2047, ...) at most 256 rows name the same one
- far_slot: int32 [8192], P('cells'), may hold values from 0 to 63
Outputs:
- adjoint: float32 [4, 2, 32768], P('freq', None, 'cells')
- gradient: float32 [32768], P('cells')
The draws below stay inside these ranges and needn't reach their ends.
Inputs may be any that keep to these rules, and one draw needn't show every extreme that they name: near_list[c, 0] = c, and every partner of c lies on the same device: near_list[c, k] // 64 == c // 64. `far_owner`: among the far pairs of one device's targets (aligned blocks of 1024 rows) at most 256 have sources on any one device.
All inputs are finite; a program needn't handle non-finite values.
Results may differ from the reference program's by a relative error of at most 0.0001.
Values sent between devices are 32-bit elements; how exact they have to be, the bound alone decides.
A program may use at most 64 MiB of HBM per device.

```python
import math
import jax
import jax.numpy as jnp
import numpy as np
from jax import lax

CLS = 64
R = 16
NEAR = 3
FAR = 16
ITERS = 2
CL_DEV = 64
CLUSTERS = 512
NCELLS = 32768
FREQS = 4
PAIRS = 8192
CAP = 256
N_CELLS = 8


def draw_near_list(key, part):
    rows = jnp.arange(CLUSTERS, dtype=jnp.int32)
    first = rows // CL_DEV * CL_DEV
    others = jax.random.randint(key, (CLUSTERS, NEAR - 1), 0, CL_DEV, dtype=jnp.int32)
    return jnp.concatenate([rows[:, None], first[:, None] + others], axis=1).astype(jnp.int32)


def with_ends(array, key, least, top_value):
    longest = array.shape.index(max(array.shape))
    spots = []
    for shift in (0, 1):
        where = [jax.random.randint(jax.random.fold_in(key, axis), (), 0, length) for axis, length in enumerate(array.shape)]
        where[longest] = (where[longest] + shift) % array.shape[longest]
        spots.append(tuple(where))
    return array.at[spots[0]].set(least).at[spots[1]].set(top_value)


def block_scale(own_key, extent, shards, low, high):
    loudness, own = 1.0, jax.random.fold_in(own_key, 6)
    for axis_at, parts in shards:
        draws = jnp.exp(jax.random.uniform(jax.random.fold_in(own, axis_at), (parts,), jnp.float32, low / len(shards), high / len(shards)))
        loudness = loudness * jnp.repeat(draws, extent[axis_at] // parts).reshape([-1 if axis == axis_at else 1 for axis in range(len(extent))])
    return loudness


def routed_block(rng, own, number, rows, number_of, top, reach, skew):
    order = jax.random.permutation(rng, number_of)
    packed, ordinary = load_shares(number_of, rows * top, reach, skew, True), load_shares(number_of, rows * top, reach, skew, False)
    places = jnp.arange(number_of)

    def named(tallies, offset_by):
        used = int((tallies > 0).sum())
        fixed = max(1, used // 4)
        moved = fixed + (places - fixed + offset_by * (used - fixed)) % max(1, number_of - fixed)
        return jnp.zeros((number_of,), jnp.int32).at[order[jnp.where(places < fixed, places, moved)]].set(jnp.asarray(tallies, jnp.int32))

    tallies = jnp.where(number % 4 == 0, named(packed, number // 4), named(ordinary, number - number // 4 - 1))
    mixed = jax.random.permutation(jax.random.fold_in(own, 3), number_of)
    source_of, receiver = mixed[0:number_of // 2 * 2:2], mixed[1:number_of // 2 * 2:2]
    slack = jnp.minimum(tallies[source_of] - 1, reach - tallies[receiver]) // 2
    slack = jnp.where((source_of == order[0]) | (receiver == order[0]) | (tallies[receiver] == 0), 0, jnp.maximum(slack, 0))
    moved = jax.random.randint(jax.random.fold_in(own, 4), (number_of // 2,), 0, 1 << 20) % (slack + 1)
    tallies = tallies.at[source_of].add(-moved).at[receiver].add(moved)
    items = jnp.searchsorted(jnp.cumsum(tallies), jnp.arange(rows * top), side="right").astype(jnp.int32)
    grid = items.reshape(top, rows).T
    grid = grid[jax.random.permutation(jax.random.fold_in(own, 1), rows)]
    offset_by = jax.random.randint(jax.random.fold_in(own, 2), (rows, 1), 0, top)
    return jnp.take_along_axis(grid, (jnp.arange(top)[None, :] + offset_by) % top, axis=1)


def load_shares(number_of, total, most, slope, full):
    portions = [(1 << 20) // math.isqrt(standing ** slope) + 1 for standing in range(1, number_of + 1)]
    largest = most if full else min(most, max(-(-total // number_of), total * portions[0] // sum(portions)))
    least = 1 if total - largest >= number_of - 1 else 0
    counts, rest = [largest] + [least] * (number_of - 1), total - largest - least * (number_of - 1)
    while rest > 0:
        movable = [i for i in range(1, number_of) if counts[i] < largest] or [i for i in range(1, number_of) if counts[i] < most]
        whole, remaining = sum([portions[i] for i in movable]), rest
        for i in movable:
            more = min(most - counts[i], max(1, remaining * portions[i] // whole), rest)
            counts[i] = counts[i] + more
            rest = rest - more
    return np.array(counts)


def normal_values(key, shape, scale, bound, pieces=(), kind=jnp.bfloat16):
    gain = block_scale(key, shape, pieces, -0.22, 0.18) if pieces else 1.0
    result = jax.random.normal(key, shape, jnp.float32) * scale * gain
    return jnp.minimum(jnp.maximum(result, -bound), bound).astype(kind)


def setup_inputs(seed: int = 0) -> dict:
    seeds = jax.random.split(jax.random.key(seed), 11)
    adj_source = normal_values(seeds[0], (FREQS, 2, NCELLS), 1.0, 6.0, ((0, 4), (2, 8)), jnp.float32)
    contrast = jnp.clip(0.2 + 0.6 * jax.random.uniform(seeds[1], (FREQS, NCELLS), jnp.float32) ** block_scale(seeds[1], (FREQS, NCELLS), ((0, 4), (1, 8)), -0.2, 0.2), 0.2, 0.8)
    background = normal_values(seeds[2], (FREQS, 2, NCELLS), 1.0, 6.0, ((0, 4), (2, 8)), jnp.float32)
    near_blocks = normal_values(seeds[3], (FREQS, 2, NEAR * CLS, NCELLS), (2 * NEAR * CLS) ** -0.5, 0.3125, ((0, 4), (3, 8)), jnp.float32)
    near_list = draw_near_list(jax.random.fold_in(seeds[10], 71), 0)
    proj_basis = normal_values(seeds[5], (FREQS, 2, R, NCELLS), (2 * CLS) ** -0.5, 0.5, ((0, 4), (3, 8)), jnp.float32)
    expand_basis = normal_values(seeds[6], (FREQS, 2, R, NCELLS), (2 * R) ** -0.5, 1.0, ((0, 4), (3, 8)), jnp.float32)
    coupling = normal_values(seeds[7], (FREQS, 2, R, R, PAIRS), (2 * R * FAR) ** -0.5, 0.25, ((0, 4), (4, 8)), jnp.float32)
    far_owner_keys = jax.random.split(jax.random.fold_in(seeds[8], 1), PAIRS // (CL_DEV * FAR))
    far_owner_turns = jax.random.permutation(jax.random.fold_in(seeds[8], 3), PAIRS // (CL_DEV * FAR))
    far_owner = jax.vmap(lambda own, number: routed_block(jax.random.fold_in(seeds[8], 2), own, number, CL_DEV * FAR, N_CELLS, 1, CAP, 2))(far_owner_keys, far_owner_turns).reshape((PAIRS, 1))
    far_slot = with_ends(jax.random.randint(seeds[9], (PAIRS,), 0, CL_DEV), jax.random.fold_in(seeds[9], 1), 0, CL_DEV - 1).astype(jnp.int32)
    return dict(adj_source=adj_source, contrast=contrast, background=background, near_blocks=near_blocks, near_list=near_list, proj_basis=proj_basis, expand_basis=expand_basis, coupling=coupling, far_owner=far_owner, far_slot=far_slot)


def apply_green(f, field, contrast, near_blocks, near_list, proj_basis, expand_basis, coupling, source):
    highest = lax.Precision.HIGHEST
    weighted = contrast[f][None, :] * field
    grouped = weighted.reshape(2, CLUSTERS, CLS)
    partner = grouped[:, near_list, :].reshape(2, CLUSTERS, NEAR * CLS)
    blocks = near_blocks[f].reshape(2, NEAR * CLS, CLUSTERS, CLS)

    def nearprod(a, b):
        return jnp.einsum('jct,cj->ct', a, b, precision=highest)

    near_re = nearprod(blocks[0], partner[0]) - nearprod(blocks[1], partner[1])
    near_im = nearprod(blocks[0], partner[1]) + nearprod(blocks[1], partner[0])
    basis_in = proj_basis[f].reshape(2, R, CLUSTERS, CLS)

    def project(a, b):
        return jnp.einsum('rci,ci->rc', a, b, precision=highest)

    coef_re = project(basis_in[0], grouped[0]) - project(basis_in[1], grouped[1])
    coef_im = project(basis_in[0], grouped[1]) + project(basis_in[1], grouped[0])
    pair_re = coef_re[:, source]
    pair_im = coef_im[:, source]
    mats = coupling[f]

    def couple(a, b):
        return jnp.einsum('oip,ip->op', a, b, precision=highest)

    out_re = couple(mats[0], pair_re) - couple(mats[1], pair_im)
    out_im = couple(mats[0], pair_im) + couple(mats[1], pair_re)
    out_re = out_re.reshape(R, CLUSTERS, FAR).sum(axis=2)
    out_im = out_im.reshape(R, CLUSTERS, FAR).sum(axis=2)
    basis_out = expand_basis[f].reshape(2, R, CLUSTERS, CLS)

    def expand(a, b):
        return jnp.einsum('rct,rc->ct', a, b, precision=highest)

    far_re = expand(basis_out[0], out_re) - expand(basis_out[1], out_im)
    far_im = expand(basis_out[0], out_im) + expand(basis_out[1], out_re)
    return jnp.stack([near_re + far_re, near_im + far_im]).reshape(2, NCELLS)


def reference(adj_source, contrast, background, near_blocks, near_list, proj_basis, expand_basis, coupling, far_owner, far_slot):
    source = far_owner[:, 0] * CL_DEV + far_slot
    fields = []
    for f in range(FREQS):
        field = adj_source[f]
        for step in range(ITERS):
            field = adj_source[f] + apply_green(f, field, contrast, near_blocks, near_list, proj_basis, expand_basis, coupling, source)
        fields.append(field)
    adjoint = jnp.stack(fields)
    gradient = jnp.sum(background[:, 0] * adjoint[:, 0] + background[:, 1] * adjoint[:, 1], axis=0)
    return adjoint, gradient
```

```python
import functools

import jax
import jax.numpy as jnp
from jax import lax
from jax.experimental import pallas as pl
from jax.experimental.pallas import tpu as pltpu
from jax.sharding import PartitionSpec as P

ITERS = 2
LANES = 128
MESH = pl.DeviceIdType.MESH
F32 = jnp.float32
BF16 = jnp.bfloat16


def split(x):
    high = x.astype(BF16)
    return high, (x - high.astype(F32)).astype(BF16)


def dot(a, b):
    return jnp.dot(a, b, preferred_element_type=F32)


def onehot(mask):
    return jnp.where(mask, 1.0, 0.0).astype(BF16)


def kernel(
    dims,
    adj_hbm,
    con_hbm,
    back_hbm,
    near_hbm,
    list_ref,
    proj_hbm,
    exp_hbm,
    coup_hbm,
    owner_ref,
    slot_ref,
    out_hbm,
    grad_ref,
    adj,
    con,
    back,
    near,
    proj,
    expand,
    coup,
    rows,
    spread,
    collect,
    pick_near,
    pick_far,
    pair_sum,
    acc,
    qbuf,
    gbuf,
    field,
    in_sem,
    near_sem,
    out_sem,
    send_sem,
    recv_sem,
    gsend_sem,
    grecv_sem,
):
    peers, freqs, clusters, cells, rank, near_count, pairs, near_parts = dims
    width = cells // clusters
    shift = width.bit_length() - 1
    half = LANES // 2
    lines = cells // LANES
    far_count = pairs // clusters
    far_shift = far_count.bit_length() - 1
    me = lax.axis_index("cells")
    my_f = lax.axis_index("freq")

    ins = [
        pltpu.make_async_copy(src, dst, in_sem.at[i])
        for i, (src, dst) in enumerate(
            [(con_hbm, con), (adj_hbm, adj), (proj_hbm, proj), (coup_hbm, coup), (exp_hbm, expand), (back_hbm, back)]
        )
    ]
    con_in, adj_in, proj_in, coup_in, exp_in, back_in = ins
    part = cells // near_parts
    near_in = [
        pltpu.make_async_copy(
            near_hbm.at[:, :, pl.ds(i * part, part)], near.at[:, :, pl.ds(i * part, part)], near_sem.at[i]
        )
        for i in range(near_parts)
    ]
    con_in.start()
    adj_in.start()
    proj_in.start()
    for c in near_in:
        c.start()
    coup_in.start()
    exp_in.start()
    back_in.start()

    barrier = pltpu.get_barrier_semaphore()
    for d in range(1, peers):
        pl.semaphore_signal(barrier, inc=1, device_id={"cells": lax.rem(me + d, peers)}, device_id_type=MESH)
    for d in range(1, freqs):
        pl.semaphore_signal(barrier, inc=1, device_id={"freq": lax.rem(my_f + d, freqs)}, device_id_type=MESH)

    step = 512
    for t in range(0, cells, step):
        r = lax.broadcasted_iota(jnp.int32, (LANES, step), 0) & (half - 1)
        c = (lax.broadcasted_iota(jnp.int32, (LANES, step), 1) + t) >> shift
        spread[:, t : t + step] = onehot(r == c)
        r = (lax.broadcasted_iota(jnp.int32, (step, LANES), 0) + t) >> shift
        c = lax.broadcasted_iota(jnp.int32, (step, LANES), 1) & (half - 1)
        collect[t : t + step, :] = onehot(r == c)

    lane64 = lax.broadcasted_iota(jnp.int32, (rank, LANES), 1) < half

    def weigh():
        w = field[:, :] * con[:, :]
        high = w.astype(BF16).astype(F32)
        low = w - high
        for ri in range(2):
            for m in range(lines):
                rows[ri * lines + m : ri * lines + m + 1, :] = high[ri : ri + 1, m * LANES : (m + 1) * LANES]
                rows[(2 + ri) * lines + m : (2 + ri) * lines + m + 1, :] = low[ri : ri + 1, m * LANES : (m + 1) * LANES]
        return w

    def project(w, it):
        total = jnp.zeros((4 * rank, LANES), F32)
        for t in range(0, cells, step):
            wr, wi = w[0:1, t : t + step], w[1:2, t : t + step]
            pr, pi = proj[0, :, t : t + step], proj[1, :, t : t + step]
            re_h, re_l = split(pr * wr - pi * wi)
            im_h, im_l = split(pr * wi + pi * wr)
            x = jnp.concatenate([re_h, im_h, re_l, im_l], axis=0)
            total += dot(x, collect[t : t + step, :])
        q = total[: 2 * rank] + total[2 * rank :]
        qbuf[it, me] = jnp.where(lane64, q[:rank], q[rank:])

    def send(it):
        sends = []
        for d in range(1, peers):
            copy = pltpu.make_async_remote_copy(
                src_ref=qbuf.at[it, me],
                dst_ref=qbuf.at[it, me],
                send_sem=send_sem.at[it, d],
                recv_sem=recv_sem.at[it, d],
                device_id={"cells": lax.rem(me + d, peers)},
                device_id_type=MESH,
            )
            copy.start()
            sends.append(copy)
        return sends

    def near_field(it):
        turned = rows[:, :].T.astype(BF16)
        left = jnp.concatenate([turned[:width], turned[width:]], axis=1)
        got = dot(left, pick_near[:, :])
        lane = lax.broadcasted_iota(jnp.int32, (width, LANES), 1) < half
        parts = []
        for b in range(2 * near_count):
            g = got[:, b * LANES : (b + 1) * LANES]
            high = g.astype(BF16).astype(F32)
            parts.append(jnp.where(lane, high, g - high).astype(BF16))
        lhs = jnp.concatenate(parts, axis=0)
        deep = near_count * width
        chunk = 256

        def one(t):
            at = pl.ds(pl.multiple_of(t * chunk, chunk), chunk)
            wide = dot(lhs, spread[:, at])
            re = jnp.zeros((8, chunk), F32)
            im = jnp.zeros((8, chunk), F32)
            for j in range(0, deep, 8):
                br, bi = near[0, j : j + 8, at], near[1, j : j + 8, at]
                wr, wi = wide[j : j + 8], wide[deep + j : deep + j + 8]
                re += br * wr - bi * wi
                im += br * wi + bi * wr
            acc[0, :, at] = re
            acc[1, :, at] = im

        per = part // chunk
        if it == 0:
            for i in range(near_parts):
                near_in[i].wait()
                pl.loop(i * per, (i + 1) * per)(one)
        else:
            pl.loop(0, cells // chunk)(one)

    def far_field(it, sends):
        for c in sends:
            c.wait_recv()
        re, im = [], []
        for m in range(0, peers, 2):
            a, b = qbuf[it, m], qbuf[it, m + 1]
            re.append(jnp.where(lane64, a, pltpu.roll(b, half, 1)))
            im.append(jnp.where(lane64, pltpu.roll(a, half, 1), b))
        q = jnp.concatenate([jnp.concatenate(re, axis=1), jnp.concatenate(im, axis=1)], axis=0)
        q_h, q_l = split(q)
        got = dot(jnp.concatenate([q_h, q_l], axis=0), pick_far[:, :])
        got = got[: 2 * rank] + got[2 * rank :]
        qr, qi = got[:rank], got[rank:]
        if it == 0:
            coup_in.wait()
        sums = jnp.zeros((2 * rank * 8, LANES), F32)
        wide = 256
        for t in range(0, pairs, wide):
            res, ims = [], []
            a, b = qr[:, t : t + wide], qi[:, t : t + wide]
            for o in range(rank):
                cr, ci = coup[0, o, :, t : t + wide], coup[1, o, :, t : t + wide]
                x = cr * a - ci * b
                y = cr * b + ci * a
                res.append(sum(x[k : k + 8] for k in range(0, rank, 8)))
                ims.append(sum(y[k : k + 8] for k in range(0, rank, 8)))
            high, low = split(jnp.concatenate(res + ims, axis=0))
            sel = pair_sum[t : t + wide, :]
            sums += dot(high, sel) + dot(low, sel)
        z = jnp.sum(sums.reshape(2 * rank, 8, LANES), axis=1)
        z_high = z.astype(BF16).astype(F32)
        lane = lax.broadcasted_iota(jnp.int32, (2 * rank, LANES), 1) < half
        z = jnp.where(lane, z_high, z - z_high).astype(BF16)
        if it == 0:
            exp_in.wait()
        for t in range(0, cells, step):
            wide_z = dot(z, spread[:, t : t + step])
            zr, zi = wide_z[:rank], wide_z[rank:]
            er, ei = expand[0, :, t : t + step], expand[1, :, t : t + step]
            x = er * zr - ei * zi
            y = er * zi + ei * zr
            x = acc[0, :, t : t + step] + sum(x[k : k + 8] for k in range(0, rank, 8))
            y = acc[1, :, t : t + step] + sum(y[k : k + 8] for k in range(0, rank, 8))
            new = jnp.concatenate([jnp.sum(x, axis=0, keepdims=True), jnp.sum(y, axis=0, keepdims=True)], axis=0)
            field[:, t : t + step] = adj[:, t : t + step] + new

    con_in.wait()
    adj_in.wait()
    field[:, :] = adj[:, :]
    w = weigh()
    proj_in.wait()
    project(w, 0)
    pl.semaphore_wait(barrier, peers + freqs - 2)
    sends = send(0)
    everyone = sends

    r = lax.broadcasted_iota(jnp.int32, (2 * LANES, LANES), 0)
    lbits = lines.bit_length() - 1
    cluster = ((r & (lines - 1)) << 1) + (r >> 7)
    source_ri = (r >> lbits) & 1
    local = list_ref[:, :] - me * clusters
    local = jnp.concatenate([local, local], axis=1)
    for ri in range(2):
        for k in range(near_count):
            b = ri * near_count + k
            pick_near[:, b * LANES : (b + 1) * LANES] = onehot((cluster == local[k : k + 1, :]) & (source_ri == ri))
    near_field(0)

    source = owner_ref[:, :] * clusters + slot_ref[:, :]

    @pl.loop(0, peers * clusters // 64)
    def _(i):
        r = lax.broadcasted_iota(jnp.int32, (64, pairs), 0) + i * 64
        pick_far[pl.ds(pl.multiple_of(i * 64, 64), 64), :] = onehot(r == source)

    r = lax.broadcasted_iota(jnp.int32, (pairs, LANES), 0) >> far_shift
    c = lax.broadcasted_iota(jnp.int32, (pairs, LANES), 1) & (half - 1)
    pair_sum[:, :] = onehot(r == c)

    far_field(0, sends)
    for it in range(1, ITERS):
        w = weigh()
        project(w, it)
        sends = send(it)
        everyone = everyone + sends
        near_field(it)
        far_field(it, sends)

    out_copy = pltpu.make_async_copy(field, out_hbm, out_sem)
    out_copy.start()
    back_in.wait()
    terms = back[:, :] * field[:, :]
    terms = terms[0:1] + terms[1:2]
    for m in range(lines):
        gbuf[0, m : m + 1, :] = terms[:, m * LANES : (m + 1) * LANES]
    gsends = []
    for d in range(1, freqs):
        copy = pltpu.make_async_remote_copy(
            src_ref=gbuf.at[0],
            dst_ref=gbuf.at[d],
            send_sem=gsend_sem.at[d],
            recv_sem=grecv_sem.at[d],
            device_id={"freq": lax.rem(my_f + d, freqs)},
            device_id_type=MESH,
        )
        copy.start()
        gsends.append(copy)
    for c in everyone:
        c.wait_send()
    total = gbuf[0]
    for d, c in enumerate(gsends):
        c.wait_recv()
        total += gbuf[d + 1]
    grad_ref[:, :] = total
    for c in gsends:
        c.wait_send()
    out_copy.wait()


def per_device(
    peers,
    freqs,
    adj_source,
    contrast,
    background,
    near_blocks,
    near_list,
    proj_basis,
    expand_basis,
    coupling,
    far_owner,
    far_slot,
):
    clusters, near_count = near_list.shape
    cells = contrast.shape[1]
    rank = proj_basis.shape[2]
    pairs = far_slot.shape[0]
    lines = cells // LANES
    near_parts = 4
    dims = (peers, freqs, clusters, cells, rank, near_count, pairs, near_parts)
    hbm = pl.BlockSpec(memory_space=pl.ANY)
    vmem = pl.BlockSpec(memory_space=pltpu.VMEM)
    deep = near_blocks.shape[2]
    adjoint, gradient = pl.pallas_call(
        functools.partial(kernel, dims),
        out_shape=(
            jax.ShapeDtypeStruct((2, cells), F32),
            jax.ShapeDtypeStruct((lines, LANES), F32),
        ),
        in_specs=[hbm, hbm, hbm, hbm, vmem, hbm, hbm, hbm, vmem, vmem],
        out_specs=(hbm, vmem),
        scratch_shapes=[
            pltpu.VMEM((2, cells), F32),
            pltpu.VMEM((1, cells), F32),
            pltpu.VMEM((2, cells), F32),
            pltpu.VMEM((2, deep, cells), F32),
            pltpu.VMEM((2, rank, cells), F32),
            pltpu.VMEM((2, rank, cells), F32),
            pltpu.VMEM((2, rank, rank, pairs), F32),
            pltpu.VMEM((4 * lines, LANES), F32),
            pltpu.VMEM((LANES, cells), BF16),
            pltpu.VMEM((cells, LANES), BF16),
            pltpu.VMEM((2 * LANES, 2 * near_count * LANES), BF16),
            pltpu.VMEM((peers * clusters, pairs), BF16),
            pltpu.VMEM((pairs, LANES), BF16),
            pltpu.VMEM((2, 8, cells), F32),
            pltpu.VMEM((ITERS, peers, rank, LANES), F32),
            pltpu.VMEM((freqs, lines, LANES), F32),
            pltpu.VMEM((2, cells), F32),
            pltpu.SemaphoreType.DMA((6,)),
            pltpu.SemaphoreType.DMA((near_parts,)),
            pltpu.SemaphoreType.DMA,
            pltpu.SemaphoreType.DMA((ITERS, peers)),
            pltpu.SemaphoreType.DMA((ITERS, peers)),
            pltpu.SemaphoreType.DMA((freqs,)),
            pltpu.SemaphoreType.DMA((freqs,)),
        ],
        compiler_params=pltpu.CompilerParams(
            collective_id=0, has_side_effects=True, vmem_limit_bytes=48 * 2**20
        ),
    )(
        adj_source[0],
        contrast,
        background[0],
        near_blocks[0],
        near_list.T,
        proj_basis[0],
        expand_basis[0],
        coupling[0],
        far_owner.reshape(1, pairs),
        far_slot.reshape(1, pairs),
    )
    return adjoint[None], gradient.reshape(cells)


def solution(mesh):
    return jax.shard_map(
        functools.partial(per_device, mesh.shape["cells"], mesh.shape["freq"]),
        mesh=mesh,
        in_specs=(
            P("freq", None, "cells"),
            P("freq", "cells"),
            P("freq", None, "cells"),
            P("freq", None, None, "cells"),
            P("cells", None),
            P("freq", None, None, "cells"),
            P("freq", None, None, "cells"),
            P("freq", None, None, None, "cells"),
            P("cells", None),
            P("cells"),
        ),
        out_specs=(P("freq", None, "cells"), P("cells")),
        check_vma=False,
    )
```

```python
import functools

import jax
import jax.numpy as jnp
from jax import lax
from jax.experimental import pallas as pl
from jax.experimental.pallas import tpu as pltpu
from jax.sharding import PartitionSpec as P

ITERS = 2
LANES = 128
MESH = pl.DeviceIdType.MESH
F32 = jnp.float32
BF16 = jnp.bfloat16


def split(x):
    high = x.astype(BF16)
    return high, (x - high.astype(F32)).astype(BF16)


def dot(a, b):
    return jnp.dot(a, b, preferred_element_type=F32)


def onehot(mask):
    return jnp.where(mask, 1.0, 0.0).astype(BF16)


def kernel(
    dims,
    adj_hbm,
    con_hbm,
    back_hbm,
    near_hbm,
    list_hbm,
    proj_hbm,
    exp_hbm,
    coup_hbm,
    owner_hbm,
    slot_hbm,
    out_hbm,
    grad_ref,
    adj,
    con,
    back,
    near,
    proj,
    expand,
    coup,
    list_ref,
    owner_ref,
    slot_ref,
    rows,
    wbuf,
    spread,
    collect,
    pick_near,
    left,
    block_h,
    block_l,
    pick_far,
    pair_sum,
    acc,
    qbuf,
    gbuf,
    field,
    in_sem,
    near_sem,
    out_sem,
    send_sem,
    recv_sem,
    gsend_sem,
    grecv_sem,
):
    peers, freqs, clusters, cells, rank, near_count, pairs, near_parts = dims
    width = cells // clusters
    shift = width.bit_length() - 1
    half = LANES // 2
    lines = cells // LANES
    far_count = pairs // clusters
    far_shift = far_count.bit_length() - 1
    me = lax.axis_index("cells")
    my_f = lax.axis_index("freq")

    ins = [
        pltpu.make_async_copy(src, dst, in_sem.at[i])
        for i, (src, dst) in enumerate(
            [(con_hbm, con), (adj_hbm, adj), (proj_hbm, proj), (coup_hbm, coup), (exp_hbm, expand), (back_hbm, back), (list_hbm, list_ref), (owner_hbm, owner_ref), (slot_hbm, slot_ref)]
        )
    ]
    con_in, adj_in, proj_in, coup_in, exp_in, back_in, list_in, owner_in, slot_in = ins
    part = cells // near_parts
    near_in = [
        pltpu.make_async_copy(
            near_hbm.at[:, :, pl.ds(i * part, part)], near.at[:, :, pl.ds(i * part, part)], near_sem.at[i]
        )
        for i in range(near_parts)
    ]
    con_in.start()
    adj_in.start()
    proj_in.start()
    list_in.start()
    owner_in.start()
    slot_in.start()
    for c in near_in:
        c.start()
    coup_in.start()
    exp_in.start()
    back_in.start()

    barrier = pltpu.get_barrier_semaphore()
    for d in range(1, peers):
        pl.semaphore_signal(barrier, inc=1, device_id={"cells": lax.rem(me + d, peers)}, device_id_type=MESH)
    for d in range(1, freqs):
        pl.semaphore_signal(barrier, inc=1, device_id={"freq": lax.rem(my_f + d, freqs)}, device_id_type=MESH)

    step = 512
    for t in range(0, cells, step):
        r = lax.broadcasted_iota(jnp.int32, (LANES, step), 0) & (half - 1)
        c = (lax.broadcasted_iota(jnp.int32, (LANES, step), 1) + t) >> shift
        spread[:, t : t + step] = onehot(r == c)
        r = (lax.broadcasted_iota(jnp.int32, (step, LANES), 0) + t) >> shift
        c = lax.broadcasted_iota(jnp.int32, (step, LANES), 1) & (half - 1)
        collect[t : t + step, :] = onehot(r == c)

    lane64 = lax.broadcasted_iota(jnp.int32, (rank, LANES), 1) < half

    def weigh():
        wbuf[:, :] = field[:, :] * con[:, :]
        for ri in range(2):
            for m in range(lines):
                rows[ri * lines + m : ri * lines + m + 1, :] = wbuf[ri : ri + 1, m * LANES : (m + 1) * LANES]

    def project(it):
        total = jnp.zeros((4 * rank, LANES), F32)
        for t in range(0, cells, step):
            wr, wi = wbuf[0:1, t : t + step], wbuf[1:2, t : t + step]
            pr, pi = proj[0, :, t : t + step], proj[1, :, t : t + step]
            re_h, re_l = split(pr * wr - pi * wi)
            im_h, im_l = split(pr * wi + pi * wr)
            x = jnp.concatenate([re_h, im_h, re_l, im_l], axis=0)
            total += dot(x, collect[t : t + step, :])
        q = total[: 2 * rank] + total[2 * rank :]
        qbuf[it, me] = jnp.where(lane64, q[:rank], q[rank:])

    def send(it):
        sends = []
        for d in range(1, peers):
            copy = pltpu.make_async_remote_copy(
                src_ref=qbuf.at[it, me],
                dst_ref=qbuf.at[it, me],
                send_sem=send_sem.at[it, d],
                recv_sem=recv_sem.at[it, d],
                device_id={"cells": lax.rem(me + d, peers)},
                device_id_type=MESH,
            )
            copy.start()
            sends.append(copy)
        return sends

    def near_field(it):
        first = lax.broadcasted_iota(jnp.int32, (4 * lines, LANES), 1) < half
        lined = rows[:, :]
        high = lined.astype(BF16).astype(F32)
        lined = jnp.concatenate([high, lined - high], axis=0)
        swapped = pltpu.roll(lined, half, 1)
        values = jnp.concatenate([jnp.where(first, lined, swapped), jnp.where(first, swapped, lined)], axis=0)
        values = values.astype(BF16)
        got = [dot(pick_near[k], values) for k in range(near_count)]
        first = lax.broadcasted_iota(jnp.int32, (4 * clusters, LANES), 1) < half
        left[:, :LANES] = jnp.where(first, got[0], got[1]).astype(BF16)
        left[:, LANES:] = got[2][:, :width].astype(BF16)
        chunk = 4 * width
        r = lax.broadcasted_iota(jnp.int32, (8, chunk), 0)
        c = lax.broadcasted_iota(jnp.int32, (8, chunk), 1) >> shift
        mine = (r & 3) == c
        upper = r < 4
        zero = jnp.zeros((8, chunk), F32)

        def one(t):
            at = pl.ds(pl.multiple_of(t * chunk, chunk), chunk)
            lhs = left[pl.ds(pl.multiple_of(t * 16, 16), 16), :]
            a = dot(lhs, block_h[0, :, at]) + dot(lhs, block_l[0, :, at])
            b = dot(lhs, block_h[1, :, at]) + dot(lhs, block_l[1, :, at])
            a = a[:8] + a[8:]
            b = b[:8] + b[8:]
            acc[0, :, at] = jnp.where(mine, jnp.where(upper, a, -b), zero)
            acc[1, :, at] = jnp.where(mine, jnp.where(upper, b, a), zero)

        pl.loop(0, cells // chunk, unroll=4)(one)

    def far_field(it, sends):
        for c in sends:
            c.wait_recv()
        re, im = [], []
        for m in range(0, peers, 2):
            a, b = qbuf[it, m], qbuf[it, m + 1]
            re.append(jnp.where(lane64, a, pltpu.roll(b, half, 1)))
            im.append(jnp.where(lane64, pltpu.roll(a, half, 1), b))
        q = jnp.concatenate([jnp.concatenate(re, axis=1), jnp.concatenate(im, axis=1)], axis=0)
        q_h, q_l = split(q)
        got = dot(jnp.concatenate([q_h, q_l], axis=0), pick_far[:, :])
        got = got[: 2 * rank] + got[2 * rank :]
        qr, qi = got[:rank], got[rank:]
        sums = jnp.zeros((2 * rank * 8, LANES), F32)
        wide = 256
        for t in range(0, pairs, wide):
            res, ims = [], []
            a, b = qr[:, t : t + wide], qi[:, t : t + wide]
            for o in range(rank):
                cr, ci = coup[0, o, :, t : t + wide], coup[1, o, :, t : t + wide]
                x = cr * a - ci * b
                y = cr * b + ci * a
                res.append(sum(x[k : k + 8] for k in range(0, rank, 8)))
                ims.append(sum(y[k : k + 8] for k in range(0, rank, 8)))
            high, low = split(jnp.concatenate(res + ims, axis=0))
            sel = pair_sum[t : t + wide, :]
            sums += dot(high, sel) + dot(low, sel)
        z = jnp.sum(sums.reshape(2 * rank, 8, LANES), axis=1)
        z_high = z.astype(BF16).astype(F32)
        lane = lax.broadcasted_iota(jnp.int32, (2 * rank, LANES), 1) < half
        z = jnp.where(lane, z_high, z - z_high).astype(BF16)
        for t in range(0, cells, step):
            wide_z = dot(z, spread[:, t : t + step])
            zr, zi = wide_z[:rank], wide_z[rank:]
            er, ei = expand[0, :, t : t + step], expand[1, :, t : t + step]
            x = er * zr - ei * zi
            y = er * zi + ei * zr
            x = acc[0, :, t : t + step] + sum(x[k : k + 8] for k in range(0, rank, 8))
            y = acc[1, :, t : t + step] + sum(y[k : k + 8] for k in range(0, rank, 8))
            new = jnp.concatenate([jnp.sum(x, axis=0, keepdims=True), jnp.sum(y, axis=0, keepdims=True)], axis=0)
            field[:, t : t + step] = adj[:, t : t + step] + new

    def cut(t):
        chunk = 4 * width
        at = pl.ds(pl.multiple_of(t * chunk, chunk), chunk)
        for ri in range(2):
            for j in range(0, near_count * width, 16):
                high, low = split(near[ri, j : j + 16, at])
                block_h[ri, j : j + 16, at] = high
                block_l[ri, j : j + 16, at] = low

    def prepare():
        list_in.wait()
        local = list_ref[:, :] - me * clusters
        r = lax.broadcasted_iota(jnp.int32, (4 * clusters, clusters), 0)
        c = lax.broadcasted_iota(jnp.int32, (4 * clusters, clusters), 1)
        cluster = ((r >> 4) << 2) + (r & 3)
        own = onehot(c == cluster)
        column = lax.broadcasted_iota(jnp.int32, (4 * clusters, 2 * LANES), 1)
        row = lax.broadcasted_iota(jnp.int32, (4 * clusters, 2 * LANES), 0)
        lbits = lines.bit_length() - 1
        partner = ((column & (lines - 1)) << 1) + (column >> (lbits + 2))
        same = ((row >> 2) & 3) == ((column >> lbits) & 3)
        for k in range(near_count):
            wanted = jnp.broadcast_to(local[k : k + 1, :], (LANES, clusters)).astype(F32).astype(BF16)
            wanted = lax.dot_general(own, wanted, (((1,), (1,)), ((), ())), preferred_element_type=F32)
            wanted = wanted.astype(jnp.int32)
            wanted = jnp.concatenate([wanted, wanted], axis=1)
            pick_near[k] = onehot(same & (partner == wanted))
        owner_in.wait()
        slot_in.wait()
        source = owner_ref[:, :] * clusters + slot_ref[:, :]

        @pl.loop(0, peers * clusters // 64)
        def _(i):
            r = lax.broadcasted_iota(jnp.int32, (64, pairs), 0) + i * 64
            pick_far[pl.ds(pl.multiple_of(i * 64, 64), 64), :] = onehot(r == source)

        r = lax.broadcasted_iota(jnp.int32, (pairs, LANES), 0) >> far_shift
        c = lax.broadcasted_iota(jnp.int32, (pairs, LANES), 1) & (half - 1)
        pair_sum[:, :] = onehot(r == c)

        for i in range(near_parts):
            near_in[i].wait()
            pl.loop(i * (part // (4 * width)), (i + 1) * (part // (4 * width)))(cut)
        coup_in.wait()
        exp_in.wait()

    con_in.wait()
    adj_in.wait()
    field[:, :] = adj[:, :]
    proj_in.wait()

    @pl.loop(0, ITERS)
    def _(it):
        weigh()
        project(it)

        @pl.when(it == 0)
        def _():
            pl.semaphore_wait(barrier, peers + freqs - 2)

        sends = send(it)

        @pl.when(it == 0)
        def _():
            prepare()

        near_field(it)
        far_field(it, sends)
        for c in sends:
            c.wait_send()

    out_copy = pltpu.make_async_copy(field, out_hbm, out_sem)
    out_copy.start()
    back_in.wait()
    terms = back[:, :] * field[:, :]
    wbuf[0:1, :] = terms[0:1] + terms[1:2]
    for m in range(lines):
        gbuf[0, m : m + 1, :] = wbuf[0:1, m * LANES : (m + 1) * LANES]
    gsends = []
    for d in range(1, freqs):
        copy = pltpu.make_async_remote_copy(
            src_ref=gbuf.at[0],
            dst_ref=gbuf.at[d],
            send_sem=gsend_sem.at[d],
            recv_sem=grecv_sem.at[d],
            device_id={"freq": lax.rem(my_f + d, freqs)},
            device_id_type=MESH,
        )
        copy.start()
        gsends.append(copy)
    total = gbuf[0]
    for d, c in enumerate(gsends):
        c.wait_recv()
        total += gbuf[d + 1]
    grad_ref[:, :] = total
    for c in gsends:
        c.wait_send()
    out_copy.wait()


def finish(a_ref, g_ref, a_out, g_out, a_buf, g_buf, sem):
    inward = [pltpu.make_async_copy(a_ref, a_buf, sem.at[0]), pltpu.make_async_copy(g_ref, g_buf, sem.at[1])]
    outward = [pltpu.make_async_copy(a_buf, a_out, sem.at[2]), pltpu.make_async_copy(g_buf, g_out, sem.at[3])]
    for c in inward:
        c.start()
    for c, d in zip(inward, outward):
        c.wait()
        d.start()
    for d in outward:
        d.wait()


def per_device(
    peers,
    freqs,
    adj_source,
    contrast,
    background,
    near_blocks,
    near_list,
    proj_basis,
    expand_basis,
    coupling,
    far_owner,
    far_slot,
):
    clusters, near_count = near_list.shape
    cells = contrast.shape[1]
    rank = proj_basis.shape[2]
    pairs = far_slot.shape[0]
    lines = cells // LANES
    near_parts = 4
    dims = (peers, freqs, clusters, cells, rank, near_count, pairs, near_parts)
    hbm = pl.BlockSpec(memory_space=pltpu.HBM)
    vmem = pl.BlockSpec(memory_space=pltpu.VMEM)
    deep = near_blocks.shape[2]
    adjoint, gradient = pl.pallas_call(
        functools.partial(kernel, dims),
        out_shape=(
            jax.ShapeDtypeStruct((2, cells), F32),
            jax.ShapeDtypeStruct((lines, LANES), F32),
        ),
        in_specs=[hbm] * 10,
        out_specs=(hbm, vmem),
        scratch_shapes=[
            pltpu.VMEM((2, cells), F32),
            pltpu.VMEM((1, cells), F32),
            pltpu.VMEM((2, cells), F32),
            pltpu.VMEM((2, deep, cells), F32),
            pltpu.VMEM((2, rank, cells), F32),
            pltpu.VMEM((2, rank, cells), F32),
            pltpu.VMEM((2, rank, rank, pairs), F32),
            pltpu.VMEM((near_count, clusters), jnp.int32),
            pltpu.VMEM((1, pairs), jnp.int32),
            pltpu.VMEM((1, pairs), jnp.int32),
            pltpu.VMEM((2 * lines, LANES), F32),
            pltpu.VMEM((2, cells), F32),
            pltpu.VMEM((LANES, cells), BF16),
            pltpu.VMEM((cells, LANES), BF16),
            pltpu.VMEM((near_count, 4 * clusters, 2 * LANES), BF16),
            pltpu.VMEM((4 * clusters, deep), BF16),
            pltpu.VMEM((2, deep, cells), BF16),
            pltpu.VMEM((2, deep, cells), BF16),
            pltpu.VMEM((peers * clusters, pairs), BF16),
            pltpu.VMEM((pairs, LANES), BF16),
            pltpu.VMEM((2, 8, cells), F32),
            pltpu.VMEM((ITERS, peers, rank, LANES), F32),
            pltpu.VMEM((freqs, lines, LANES), F32),
            pltpu.VMEM((2, cells), F32),
            pltpu.SemaphoreType.DMA((9,)),
            pltpu.SemaphoreType.DMA((near_parts,)),
            pltpu.SemaphoreType.DMA,
            pltpu.SemaphoreType.DMA((ITERS, peers)),
            pltpu.SemaphoreType.DMA((ITERS, peers)),
            pltpu.SemaphoreType.DMA((freqs,)),
            pltpu.SemaphoreType.DMA((freqs,)),
        ],
        compiler_params=pltpu.CompilerParams(
            collective_id=0, has_side_effects=True, vmem_limit_bytes=60 * 2**20
        ),
    )(
        adj_source[0],
        contrast,
        background[0],
        near_blocks[0],
        near_list.T,
        proj_basis[0],
        expand_basis[0],
        coupling[0],
        far_owner.reshape(1, pairs),
        far_slot.reshape(1, pairs),
    )
    adjoint, gradient = pl.pallas_call(
        finish,
        out_shape=(jax.ShapeDtypeStruct((2, cells), F32), jax.ShapeDtypeStruct((lines, LANES), F32)),
        in_specs=[hbm] * 2,
        out_specs=[hbm] * 2,
        scratch_shapes=[
            pltpu.VMEM((2, cells), F32),
            pltpu.VMEM((lines, LANES), F32),
            pltpu.SemaphoreType.DMA((4,)),
        ],
        compiler_params=pltpu.CompilerParams(vmem_limit_bytes=60 * 2**20),
    )(adjoint, gradient)
    return adjoint[None], gradient.reshape(cells)


def solution(mesh):
    return jax.shard_map(
        functools.partial(per_device, mesh.shape["cells"], mesh.shape["freq"]),
        mesh=mesh,
        in_specs=(
            P("freq", None, "cells"),
            P("freq", "cells"),
            P("freq", None, "cells"),
            P("freq", None, None, "cells"),
            P("cells", None),
            P("freq", None, None, "cells"),
            P("freq", None, None, "cells"),
            P("freq", None, None, None, "cells"),
            P("cells", None),
            P("cells"),
        ),
        out_specs=(P("freq", None, "cells"), P("cells")),
        check_vma=False,
    )
```

```python
import functools

import jax
import jax.numpy as jnp
from jax import lax
from jax.experimental import pallas as pl
from jax.experimental.pallas import tpu as pltpu
from jax.sharding import PartitionSpec as P

ITERS = 2
LANES = 128
MESH = pl.DeviceIdType.MESH
F32 = jnp.float32
BF16 = jnp.bfloat16


def split(x):
    high = x.astype(BF16)
    return high, (x - high.astype(F32)).astype(BF16)


def dot(a, b):
    return jnp.dot(a, b, preferred_element_type=F32)


def onehot(mask):
    return jnp.where(mask, 1.0, 0.0).astype(BF16)


def kernel(
    dims,
    adj_hbm,
    con_hbm,
    back_hbm,
    near_hbm,
    list_hbm,
    proj_hbm,
    exp_hbm,
    coup_hbm,
    owner_hbm,
    slot_hbm,
    out_hbm,
    grad_ref,
    adj,
    con,
    back,
    near,
    proj,
    expand,
    coup,
    list_ref,
    owner_ref,
    slot_ref,
    rows,
    wbuf,
    spread,
    collect,
    pick_near,
    left,
    block_h,
    block_l,
    pick_far,
    pair_sum,
    acc,
    qbuf,
    gbuf,
    field,
    in_sem,
    near_sem,
    out_sem,
    send_sem,
    recv_sem,
    gsend_sem,
    grecv_sem,
):
    peers, freqs, clusters, cells, rank, near_count, pairs, near_parts = dims
    width = cells // clusters
    shift = width.bit_length() - 1
    half = LANES // 2
    lines = cells // LANES
    far_count = pairs // clusters
    far_shift = far_count.bit_length() - 1
    me = lax.axis_index("cells")
    my_f = lax.axis_index("freq")

    ins = [
        pltpu.make_async_copy(src, dst, in_sem.at[i])
        for i, (src, dst) in enumerate(
            [(con_hbm, con), (adj_hbm, adj), (proj_hbm, proj), (coup_hbm, coup), (exp_hbm, expand), (back_hbm, back), (list_hbm, list_ref), (owner_hbm, owner_ref), (slot_hbm, slot_ref)]
        )
    ]
    con_in, adj_in, proj_in, coup_in, exp_in, back_in, list_in, owner_in, slot_in = ins
    part = cells // near_parts
    near_in = [
        pltpu.make_async_copy(
            near_hbm.at[:, :, pl.ds(i * part, part)], near.at[:, :, pl.ds(i * part, part)], near_sem.at[i]
        )
        for i in range(near_parts)
    ]
    con_in.start()
    adj_in.start()
    proj_in.start()
    list_in.start()
    owner_in.start()
    slot_in.start()
    for c in near_in:
        c.start()
    coup_in.start()
    exp_in.start()
    back_in.start()

    barrier = pltpu.get_barrier_semaphore()
    for d in range(1, peers):
        pl.semaphore_signal(barrier, inc=1, device_id={"cells": lax.rem(me + d, peers)}, device_id_type=MESH)
    for d in range(1, freqs):
        pl.semaphore_signal(barrier, inc=1, device_id={"freq": lax.rem(my_f + d, freqs)}, device_id_type=MESH)

    step = 512
    for t in range(0, cells, step):
        r = (lax.broadcasted_iota(jnp.int32, (step, LANES), 0) + t) >> shift
        c = lax.broadcasted_iota(jnp.int32, (step, LANES), 1) & (half - 1)
        collect[t : t + step, :] = onehot(r == c)

    lane64 = lax.broadcasted_iota(jnp.int32, (rank, LANES), 1) < half

    def weigh():
        wbuf[:, :] = field[:, :] * con[:, :]
        for ri in range(2):
            for m in range(lines):
                rows[ri * lines + m : ri * lines + m + 1, :] = wbuf[ri : ri + 1, m * LANES : (m + 1) * LANES]

    def project(it):
        total = jnp.zeros((4 * rank, LANES), F32)
        for t in range(0, cells, step):
            wr, wi = wbuf[0:1, t : t + step], wbuf[1:2, t : t + step]
            pr, pi = proj[0, :, t : t + step], proj[1, :, t : t + step]
            re_h, re_l = split(pr * wr - pi * wi)
            im_h, im_l = split(pr * wi + pi * wr)
            x = jnp.concatenate([re_h, im_h, re_l, im_l], axis=0)
            total += dot(x, collect[t : t + step, :])
        q = total[: 2 * rank] + total[2 * rank :]
        qbuf[it, me] = jnp.where(lane64, q[:rank], q[rank:])

    def send(it):
        sends = []
        for d in range(1, peers):
            copy = pltpu.make_async_remote_copy(
                src_ref=qbuf.at[it, me],
                dst_ref=qbuf.at[it, me],
                send_sem=send_sem.at[it, d],
                recv_sem=recv_sem.at[it, d],
                device_id={"cells": lax.rem(me + d, peers)},
                device_id_type=MESH,
            )
            copy.start()
            sends.append(copy)
        return sends

    def near_field(it):
        first = lax.broadcasted_iota(jnp.int32, (4 * lines, LANES), 1) < half
        lined = rows[:, :]
        high = lined.astype(BF16).astype(F32)
        lined = jnp.concatenate([high, lined - high], axis=0)
        swapped = pltpu.roll(lined, half, 1)
        values = jnp.concatenate([jnp.where(first, lined, swapped), jnp.where(first, swapped, lined)], axis=0)
        values = values.astype(BF16)
        got = [dot(pick_near[k], values) for k in range(near_count)]
        first = lax.broadcasted_iota(jnp.int32, (4 * clusters, LANES), 1) < half
        left[:, :LANES] = jnp.where(first, got[0], got[1]).astype(BF16)
        left[:, LANES:] = got[2][:, :width].astype(BF16)
        chunk = 4 * width
        r = lax.broadcasted_iota(jnp.int32, (8, chunk), 0)
        c = lax.broadcasted_iota(jnp.int32, (8, chunk), 1) >> shift
        mine = (r & 3) == c
        upper = r < 4
        zero = jnp.zeros((8, chunk), F32)

        def one(t):
            at = pl.ds(pl.multiple_of(t * chunk, chunk), chunk)
            lhs = left[pl.ds(pl.multiple_of(t * 16, 16), 16), :]
            a = dot(lhs, block_h[0, :, at]) + dot(lhs, block_l[0, :, at])
            b = dot(lhs, block_h[1, :, at]) + dot(lhs, block_l[1, :, at])
            a = a[:8] + a[8:]
            b = b[:8] + b[8:]
            acc[0, :, at] = jnp.where(mine, jnp.where(upper, a, -b), zero)
            acc[1, :, at] = jnp.where(mine, jnp.where(upper, b, a), zero)

        pl.loop(0, cells // chunk, unroll=4)(one)

    def far_field(it, sends):
        for c in sends:
            c.wait_recv()
        re, im = [], []
        for m in range(0, peers, 2):
            a, b = qbuf[it, m], qbuf[it, m + 1]
            re.append(jnp.where(lane64, a, pltpu.roll(b, half, 1)))
            im.append(jnp.where(lane64, pltpu.roll(a, half, 1), b))
        q = jnp.concatenate([jnp.concatenate(re, axis=1), jnp.concatenate(im, axis=1)], axis=0)
        q_h, q_l = split(q)
        got = dot(jnp.concatenate([q_h, q_l], axis=0), pick_far[:, :])
        got = got[: 2 * rank] + got[2 * rank :]
        qr, qi = got[:rank], got[rank:]
        sums = jnp.zeros((2 * rank * 8, LANES), F32)
        wide = 256
        for t in range(0, pairs, wide):
            res, ims = [], []
            a, b = qr[:, t : t + wide], qi[:, t : t + wide]
            for o in range(rank):
                cr, ci = coup[0, o, :, t : t + wide], coup[1, o, :, t : t + wide]
                x = cr * a - ci * b
                y = cr * b + ci * a
                res.append(sum(x[k : k + 8] for k in range(0, rank, 8)))
                ims.append(sum(y[k : k + 8] for k in range(0, rank, 8)))
            high, low = split(jnp.concatenate(res + ims, axis=0))
            sel = pair_sum[t : t + wide, :]
            sums += dot(high, sel) + dot(low, sel)
        z = jnp.sum(sums.reshape(2 * rank, 8, LANES), axis=1)
        z_high = z.astype(BF16).astype(F32)
        lane = lax.broadcasted_iota(jnp.int32, (2 * rank, LANES), 1) < half
        z = jnp.where(lane, z_high, z - z_high).astype(BF16)
        for t in range(0, cells, step):
            wide_z = dot(z, spread[:, t : t + step])
            zr, zi = wide_z[:rank], wide_z[rank:]
            er, ei = expand[0, :, t : t + step], expand[1, :, t : t + step]
            x = er * zr - ei * zi
            y = er * zi + ei * zr
            x = acc[0, :, t : t + step] + sum(x[k : k + 8] for k in range(0, rank, 8))
            y = acc[1, :, t : t + step] + sum(y[k : k + 8] for k in range(0, rank, 8))
            new = jnp.concatenate([jnp.sum(x, axis=0, keepdims=True), jnp.sum(y, axis=0, keepdims=True)], axis=0)
            field[:, t : t + step] = adj[:, t : t + step] + new

    def cut(t):
        chunk = 4 * width
        at = pl.ds(pl.multiple_of(t * chunk, chunk), chunk)
        for ri in range(2):
            for j in range(0, near_count * width, 16):
                high, low = split(near[ri, j : j + 16, at])
                block_h[ri, j : j + 16, at] = high
                block_l[ri, j : j + 16, at] = low

    def prepare():
        for t in range(0, cells, step):
            r = lax.broadcasted_iota(jnp.int32, (LANES, step), 0) & (half - 1)
            c = (lax.broadcasted_iota(jnp.int32, (LANES, step), 1) + t) >> shift
            spread[:, t : t + step] = onehot(r == c)
        list_in.wait()
        local = list_ref[:, :] - me * clusters
        r = lax.broadcasted_iota(jnp.int32, (4 * clusters, clusters), 0)
        c = lax.broadcasted_iota(jnp.int32, (4 * clusters, clusters), 1)
        cluster = ((r >> 4) << 2) + (r & 3)
        own = onehot(c == cluster)
        column = lax.broadcasted_iota(jnp.int32, (4 * clusters, 2 * LANES), 1)
        row = lax.broadcasted_iota(jnp.int32, (4 * clusters, 2 * LANES), 0)
        lbits = lines.bit_length() - 1
        partner = ((column & (lines - 1)) << 1) + (column >> (lbits + 2))
        same = ((row >> 2) & 3) == ((column >> lbits) & 3)
        for k in range(near_count):
            wanted = jnp.broadcast_to(local[k : k + 1, :], (LANES, clusters)).astype(F32).astype(BF16)
            wanted = lax.dot_general(own, wanted, (((1,), (1,)), ((), ())), preferred_element_type=F32)
            wanted = wanted.astype(jnp.int32)
            wanted = jnp.concatenate([wanted, wanted], axis=1)
            pick_near[k] = onehot(same & (partner == wanted))
        owner_in.wait()
        slot_in.wait()
        source = owner_ref[:, :] * clusters + slot_ref[:, :]

        @pl.loop(0, peers * clusters // 64)
        def _(i):
            r = lax.broadcasted_iota(jnp.int32, (64, pairs), 0) + i * 64
            pick_far[pl.ds(pl.multiple_of(i * 64, 64), 64), :] = onehot(r == source)

        r = lax.broadcasted_iota(jnp.int32, (pairs, LANES), 0) >> far_shift
        c = lax.broadcasted_iota(jnp.int32, (pairs, LANES), 1) & (half - 1)
        pair_sum[:, :] = onehot(r == c)

        for i in range(near_parts):
            near_in[i].wait()
            pl.loop(i * (part // (4 * width)), (i + 1) * (part // (4 * width)))(cut)
        coup_in.wait()
        exp_in.wait()

    con_in.wait()
    adj_in.wait()
    field[:, :] = adj[:, :]
    proj_in.wait()

    @pl.loop(0, ITERS)
    def _(it):
        weigh()
        project(it)

        @pl.when(it == 0)
        def _():
            pl.semaphore_wait(barrier, peers + freqs - 2)

        sends = send(it)

        @pl.when(it == 0)
        def _():
            prepare()

        near_field(it)
        far_field(it, sends)
        for c in sends:
            c.wait_send()

    out_copy = pltpu.make_async_copy(field, out_hbm, out_sem)
    out_copy.start()
    back_in.wait()
    terms = back[:, :] * field[:, :]
    wbuf[0:1, :] = terms[0:1] + terms[1:2]
    for m in range(lines):
        gbuf[0, m : m + 1, :] = wbuf[0:1, m * LANES : (m + 1) * LANES]
    gsends = []
    for d in range(1, freqs):
        copy = pltpu.make_async_remote_copy(
            src_ref=gbuf.at[0],
            dst_ref=gbuf.at[d],
            send_sem=gsend_sem.at[d],
            recv_sem=grecv_sem.at[d],
            device_id={"freq": lax.rem(my_f + d, freqs)},
            device_id_type=MESH,
        )
        copy.start()
        gsends.append(copy)
    total = gbuf[0]
    for d, c in enumerate(gsends):
        c.wait_recv()
        total += gbuf[d + 1]
    grad_ref[:, :] = total
    for c in gsends:
        c.wait_send()
    out_copy.wait()


def finish(a_ref, g_ref, a_out, g_out, a_buf, g_buf, sem):
    inward = [pltpu.make_async_copy(a_ref, a_buf, sem.at[0]), pltpu.make_async_copy(g_ref, g_buf, sem.at[1])]
    outward = [pltpu.make_async_copy(a_buf, a_out, sem.at[2]), pltpu.make_async_copy(g_buf, g_out, sem.at[3])]
    for c in inward:
        c.start()
    for c, d in zip(inward, outward):
        c.wait()
        d.start()
    for d in outward:
        d.wait()


def per_device(
    peers,
    freqs,
    adj_source,
    contrast,
    background,
    near_blocks,
    near_list,
    proj_basis,
    expand_basis,
    coupling,
    far_owner,
    far_slot,
):
    clusters, near_count = near_list.shape
    cells = contrast.shape[1]
    rank = proj_basis.shape[2]
    pairs = far_slot.shape[0]
    lines = cells // LANES
    near_parts = 4
    dims = (peers, freqs, clusters, cells, rank, near_count, pairs, near_parts)
    hbm = pl.BlockSpec(memory_space=pltpu.HBM)
    vmem = pl.BlockSpec(memory_space=pltpu.VMEM)
    deep = near_blocks.shape[2]
    adjoint, gradient = pl.pallas_call(
        functools.partial(kernel, dims),
        out_shape=(
            jax.ShapeDtypeStruct((2, cells), F32),
            jax.ShapeDtypeStruct((lines, LANES), F32),
        ),
        in_specs=[hbm] * 10,
        out_specs=(hbm, vmem),
        scratch_shapes=[
            pltpu.VMEM((2, cells), F32),
            pltpu.VMEM((1, cells), F32),
            pltpu.VMEM((2, cells), F32),
            pltpu.VMEM((2, deep, cells), F32),
            pltpu.VMEM((2, rank, cells), F32),
            pltpu.VMEM((2, rank, cells), F32),
            pltpu.VMEM((2, rank, rank, pairs), F32),
            pltpu.VMEM((near_count, clusters), jnp.int32),
            pltpu.VMEM((1, pairs), jnp.int32),
            pltpu.VMEM((1, pairs), jnp.int32),
            pltpu.VMEM((2 * lines, LANES), F32),
            pltpu.VMEM((2, cells), F32),
            pltpu.VMEM((LANES, cells), BF16),
            pltpu.VMEM((cells, LANES), BF16),
            pltpu.VMEM((near_count, 4 * clusters, 2 * LANES), BF16),
            pltpu.VMEM((4 * clusters, deep), BF16),
            pltpu.VMEM((2, deep, cells), BF16),
            pltpu.VMEM((2, deep, cells), BF16),
            pltpu.VMEM((peers * clusters, pairs), BF16),
            pltpu.VMEM((pairs, LANES), BF16),
            pltpu.VMEM((2, 8, cells), F32),
            pltpu.VMEM((ITERS, peers, rank, LANES), F32),
            pltpu.VMEM((freqs, lines, LANES), F32),
            pltpu.VMEM((2, cells), F32),
            pltpu.SemaphoreType.DMA((9,)),
            pltpu.SemaphoreType.DMA((near_parts,)),
            pltpu.SemaphoreType.DMA,
            pltpu.SemaphoreType.DMA((ITERS, peers)),
            pltpu.SemaphoreType.DMA((ITERS, peers)),
            pltpu.SemaphoreType.DMA((freqs,)),
            pltpu.SemaphoreType.DMA((freqs,)),
        ],
        compiler_params=pltpu.CompilerParams(
            collective_id=0, has_side_effects=True, vmem_limit_bytes=60 * 2**20
        ),
    )(
        adj_source[0],
        contrast,
        background[0],
        near_blocks[0],
        near_list.T,
        proj_basis[0],
        expand_basis[0],
        coupling[0],
        far_owner.reshape(1, pairs),
        far_slot.reshape(1, pairs),
    )
    adjoint, gradient = pl.pallas_call(
        finish,
        out_shape=(jax.ShapeDtypeStruct((2, cells), F32), jax.ShapeDtypeStruct((lines, LANES), F32)),
        in_specs=[hbm] * 2,
        out_specs=[hbm] * 2,
        scratch_shapes=[
            pltpu.VMEM((2, cells), F32),
            pltpu.VMEM((lines, LANES), F32),
            pltpu.SemaphoreType.DMA((4,)),
        ],
        compiler_params=pltpu.CompilerParams(vmem_limit_bytes=60 * 2**20),
    )(adjoint, gradient)
    return adjoint[None], gradient.reshape(cells)


def solution(mesh):
    return jax.shard_map(
        functools.partial(per_device, mesh.shape["cells"], mesh.shape["freq"]),
        mesh=mesh,
        in_specs=(
            P("freq", None, "cells"),
            P("freq", "cells"),
            P("freq", None, "cells"),
            P("freq", None, None, "cells"),
            P("cells", None),
            P("freq", None, None, "cells"),
            P("freq", None, None, "cells"),
            P("freq", None, None, None, "cells"),
            P("cells", None),
            P("cells"),
        ),
        out_specs=(P("freq", None, "cells"), P("cells")),
        check_vma=False,
    )
```
